512 devices in a mesh: frame: 32 (over z_hi, y), height: 16 (over x, z_lo, core).
Axes of the slice: x: 4, y: 8, z: 8 (z_hi: 4, z_lo: 2; z = z_hi * 2 + z_lo), core: 2. Of those that a mesh axis runs over, the one named last changes fastest.
Arguments:
- queries: bfloat16 [32, 32, 80, 256], P('frame', 'height'), may hold values from -100 to 100
- keys: bfloat16 [32, 32, 80, 256], P('frame', 'height'), may hold values from -6 to 6
- values: bfloat16 [32, 32, 80, 256], P('frame', 'height'), may hold values from -6 to 6
- d_out: bfloat16 [32, 32, 80, 256], P('frame', 'height'), may hold values from -6 to 6
- reach: int32 [32, 16, 2, 2], P('frame', 'height'), may hold values from 0 to 1
Outputs:
- attended: bfloat16 [32, 32, 80, 256], P('frame', 'height')
- grad_queries: bfloat16 [32, 32, 80, 256], P('frame', 'height')
- grad_keys: bfloat16 [32, 32, 80, 256], P('frame', 'height')
- grad_values: bfloat16 [32, 32, 80, 256], P('frame', 'height')
The draws below stay inside these ranges and needn't reach their ends.
All inputs are finite; a program needn't handle non-finite values.
Results may differ from the reference program's by a relative error of at most 0.04.
Values may be sent and summed in bfloat16 or wider, within the bound.
No kernel may reach another device: no remote copies, remote signals or barrier semaphores. Data moves between devices by JAX's collectives and lax.ppermute only.
A program may use at most 64 MiB of HBM per device.

```python
import jax
import jax.numpy as jnp
from jax import lax

HEADS = 2
HD = 128
FR_DEV = 1
HR_DEV = 2
W = 80
WT = 8
FRAMES = 32
HEIGHT = 32
N_FRAME = 32
N_HEIGHT = 16


def shared_keys(key):
    return jnp.clip(jax.random.normal(key, (FRAMES, HEIGHT, W, HEADS * HD), jnp.float32), -5.0, 5.0)


def draw_keys(key, part):
    base = shared_keys(key)
    return base.astype(jnp.bfloat16)


def draw_queries(key, part):
    base = shared_keys(key)
    key = jax.random.fold_in(key, 5)
    fresh = jnp.clip(jax.random.normal(key, base.shape, jnp.float32), -6.0, 6.0)
    return fresh.astype(jnp.bfloat16)


def touch_ends(values, own_key, least, top_value):
    place = [jax.random.randint(jax.random.fold_in(own_key, axis), (), 0, length) for axis, length in enumerate(values.shape)]
    longest = values.shape.index(max(values.shape))
    neighbour = place[:longest] + [(place[longest] + 1) % values.shape[longest]] + place[longest + 1:]
    return values.at[tuple(place)].set(least).at[tuple(neighbour)].set(top_value)


def shard_levels(key, extent, cuts, least, largest):
    level, own = 1.0, jax.random.fold_in(key, 6)
    for dim, parts in cuts:
        draws = jnp.exp(jax.random.uniform(jax.random.fold_in(own, dim), (parts,), jnp.float32, least / len(cuts), largest / len(cuts)))
        level = level * jnp.repeat(draws, extent[dim] // parts).reshape([-1 if axis == dim else 1 for axis in range(len(extent))])
    return level


def normal_values(own_key, dims, scale, limit, cuts=(), kind=jnp.bfloat16):
    entries = jax.random.normal(own_key, dims, jnp.float32) * scale
    if len(cuts) > 0:
        entries = shard_levels(own_key, dims, cuts, -0.22, 0.18) * entries
    return jnp.clip(entries, min=-limit, max=limit).astype(kind)


def setup_inputs(seed: int = 0) -> dict:
    seeds = jax.random.split(jax.random.key(seed), 6)
    return {
        "queries": draw_queries(jax.random.fold_in(seeds[5], 71), 0),
        "keys": draw_keys(jax.random.fold_in(seeds[5], 71), 0),
        "values": normal_values(seeds[2], (FRAMES, HEIGHT, W, HEADS * HD), 1.0, 6.0, ((0, 32), (1, 16))),
        "d_out": normal_values(seeds[3], (FRAMES, HEIGHT, W, HEADS * HD), 1.0, 6.0, ((0, 32), (1, 16))),
        "reach": touch_ends(jax.random.randint(seeds[4], (N_FRAME, N_HEIGHT, HEADS, 2), 0, 2), jax.random.fold_in(seeds[4], 1), 0, 1).astype(jnp.int32),
    }


def to_tiles(array):
    chans = array.shape[-1]
    split = array.reshape(N_FRAME, FR_DEV, N_HEIGHT, HR_DEV, W, chans)
    return split.transpose(0, 2, 1, 3, 4, 5).reshape(N_FRAME, N_HEIGHT, FR_DEV * HR_DEV * W, chans)


def from_tiles(array):
    chans = array.shape[-1]
    split = array.reshape(N_FRAME, N_HEIGHT, FR_DEV, HR_DEV, W, chans)
    return split.transpose(0, 2, 1, 3, 4, 5).reshape(FRAMES, HEIGHT, W, chans)


def reference(queries, keys, values, d_out, reach):
    tok_count = FR_DEV * HR_DEV * W
    chans = HEADS * HD
    score_scale = HD ** -0.5
    q_tiles = to_tiles(queries)
    k_pad = jnp.pad(to_tiles(keys), ((1, 1), (1, 1), (0, 0), (0, 0)))
    v_pad = jnp.pad(to_tiles(values), ((1, 1), (1, 1), (0, 0), (0, 0)))
    o_tiles = to_tiles(d_out)
    groups = (jnp.arange(tok_count, dtype=jnp.int32) % W) // WT
    near_cols = jnp.abs(groups[:, None] - groups[None, :]) <= 1
    wide_cols = jnp.tile(near_cols, (1, 9))
    frame_step = jnp.repeat(jnp.arange(3, dtype=jnp.int32) - 1, 3)
    height_step = jnp.tile(jnp.arange(3, dtype=jnp.int32) - 1, 3)
    zero_index = jnp.zeros((), jnp.int32)
    empty = jnp.zeros(k_pad.shape, jnp.float32)

    def one_tile(carry, position):
        grad_k_acc, grad_v_acc = carry
        tile_frame = (position // N_HEIGHT).astype(jnp.int32)
        tile_height = (position % N_HEIGHT).astype(jnp.int32)
        start = (tile_frame, tile_height, zero_index, zero_index)
        k_near = lax.dynamic_slice(k_pad, start, (3, 3, tok_count, chans)).reshape(9 * tok_count, HEADS, HD)
        v_near = lax.dynamic_slice(v_pad, start, (3, 3, tok_count, chans)).reshape(9 * tok_count, HEADS, HD)
        q_here = q_tiles[tile_frame, tile_height].reshape(tok_count, HEADS, HD)
        o_here = o_tiles[tile_frame, tile_height].reshape(tok_count, HEADS, HD)
        reach_here = reach[tile_frame, tile_height]
        ingrid = (tile_frame + frame_step >= 0) & (tile_frame + frame_step < N_FRAME)
        ingrid = ingrid & (tile_height + height_step >= 0) & (tile_height + height_step < N_HEIGHT)
        tile_ok = ingrid[None, :] & (jnp.abs(frame_step)[None, :] <= reach_here[:, 0:1]) & (jnp.abs(height_step)[None, :] <= reach_here[:, 1:2])
        mask = jnp.repeat(tile_ok, tok_count, axis=1)[:, None, :] & wide_cols[None]
        q_float = q_here.astype(jnp.float32)
        k_float = k_near.astype(jnp.float32)
        v_float = v_near.astype(jnp.float32)
        o_float = o_here.astype(jnp.float32)
        scores = jnp.einsum("qhd,khd->hqk", q_float, k_float) * score_scale
        row_max = jnp.max(jnp.where(mask, scores, -jnp.inf), axis=-1, keepdims=True)
        weights = jnp.where(mask, jnp.exp(scores - row_max), 0.0)
        probs = weights / jnp.sum(weights, axis=-1, keepdims=True)
        probs_b = lax.optimization_barrier(probs.astype(jnp.bfloat16)).astype(jnp.float32)
        attended = jnp.einsum("hqk,khd->qhd", probs_b, v_float).astype(jnp.bfloat16)
        delta = jnp.einsum("qhd,qhd->hq", o_float, attended.astype(jnp.float32))
        grad_probs = jnp.einsum("qhd,khd->hqk", o_float, v_float)
        grad_scores = lax.optimization_barrier((probs * (grad_probs - delta[:, :, None]) * score_scale).astype(jnp.bfloat16)).astype(jnp.float32)
        grad_q = jnp.einsum("hqk,khd->qhd", grad_scores, k_float).astype(jnp.bfloat16)
        grad_k_part = jnp.einsum("hqk,qhd->khd", grad_scores, q_float).reshape(3, 3, tok_count, chans)
        grad_v_part = jnp.einsum("hqk,qhd->khd", probs_b, o_float).reshape(3, 3, tok_count, chans)
        grad_k_acc = lax.dynamic_update_slice(grad_k_acc, lax.dynamic_slice(grad_k_acc, start, (3, 3, tok_count, chans)) + grad_k_part, start)
        grad_v_acc = lax.dynamic_update_slice(grad_v_acc, lax.dynamic_slice(grad_v_acc, start, (3, 3, tok_count, chans)) + grad_v_part, start)
        return (grad_k_acc, grad_v_acc), (attended.reshape(tok_count, chans), grad_q.reshape(tok_count, chans))

    positions = jnp.arange(N_FRAME * N_HEIGHT, dtype=jnp.int32)
    (grad_k_acc, grad_v_acc), (att_tiles, gq_tiles) = lax.scan(one_tile, (empty, empty), positions)
    attended = from_tiles(att_tiles.reshape(N_FRAME, N_HEIGHT, tok_count, chans))
    grad_queries = from_tiles(gq_tiles.reshape(N_FRAME, N_HEIGHT, tok_count, chans))
    grad_keys = from_tiles(grad_k_acc[1:-1, 1:-1].astype(jnp.bfloat16))
    grad_values = from_tiles(grad_v_acc[1:-1, 1:-1].astype(jnp.bfloat16))
    return attended, grad_queries, grad_keys, grad_values
```

```python
import functools

import jax
import jax.numpy as jnp
from jax import lax
from jax.experimental import pallas as pl
from jax.experimental.pallas import tpu as pltpu
from jax.sharding import PartitionSpec as P

W = 80
WT = 8
GROUPS = W // WT
TOK = 160
HEADS = 2
HD = 128
CHANS = HEADS * HD
BLOCKS = W // 16
SPAN = 288
KEYS = 1440
PADDED = 1536
TILE = 256
NEG = -1e30
LOG2E = 1.4426950408889634
BOTH = ("frame", "height")


def tile_groups():
    found = []
    for m in range(PADDED // TILE):
        lo, hi = m * TILE, min((m + 1) * TILE, KEYS)
        first, last = lo // SPAN, (hi - 1) // SPAN
        found.append((max(2 * first - 1, 0), min(2 * last + 2, GROUPS - 1)))
    return found


TILE_GROUPS = tile_groups()
GROUP_TILES = [
    [m for m, (a, b) in enumerate(TILE_GROUPS) if a <= g <= b] for g in range(GROUPS)
]


def dot_nt(a, b):
    return lax.dot_general(a, b, (((1,), (1,)), ((), ())), preferred_element_type=jnp.float32)


def dot_nn(a, b):
    return lax.dot_general(a, b, (((1,), (0,)), ((), ())), preferred_element_type=jnp.float32)


def dot_tn(a, b):
    return lax.dot_general(a, b, (((0,), (0,)), ((), ())), preferred_element_type=jnp.float32)


def by_group(ref):
    wide = ref[...].astype(jnp.float32)
    parts = []
    for g in range(GROUPS):
        for r in range(2):
            parts.append(wide[r * W + g * WT : r * W + (g + 1) * WT])
    return jnp.concatenate(parts, axis=0).astype(jnp.bfloat16)


def by_row(wide):
    parts = []
    for r in range(2):
        for g in range(GROUPS):
            parts.append(wide[g * 16 + r * WT : g * 16 + (r + 1) * WT])
    return jnp.concatenate(parts, axis=0).astype(jnp.bfloat16)


def attn_kernel(
    nframe, nheight,
    reach, q, o, x, xe, xf, xo, xeo, xfo, xp,
    att, gq, ge, geo, gfo_, go, gfe, gfo, gown,
    qs, os_, ks, vs, sc, dp, pb, ds, gk, gv, aacc, qacc,
):
    frame, height = lax.axis_index("frame"), lax.axis_index("height")
    fo_ok = (frame > 0) & (frame < nframe - 1)
    o_ok = (height > 0) & (height < nheight - 1)
    slots = [(x, 0), (xp, 0), (xo, 0), (xe, 0), (xp, 2), (xeo, 0), (xf, 0), (xp, 4), (xfo, 0)]
    for slot, (ref, at) in enumerate(slots):
        for j in range(BLOCKS):
            for r in range(2):
                row = j * SPAN + (slot * 2 + r) * 16
                src = slice(r * W + 16 * j, r * W + 16 * j + 16)
                ks[row : row + 16] = ref[at, src]
                vs[row : row + 16] = ref[at + 1, src]
    ks[KEYS:] = jnp.zeros((PADDED - KEYS, CHANS), jnp.bfloat16)
    vs[KEYS:] = jnp.zeros((PADDED - KEYS, CHANS), jnp.bfloat16)
    qs[...] = by_group(q)
    os_[...] = by_group(o)

    key = lax.broadcasted_iota(jnp.int32, (1, PADDED), 1)
    block = key // SPAN
    within = key - block * SPAN
    key_row = within // 16
    key_group = jnp.where(key < KEYS, block * 2 + (within % 16) // WT, 1000)
    slot_of = key_row // 2
    a_of, b_of = slot_of // 3, slot_of % 3

    scale = HD ** (-0.5)
    for h in range(HEADS):
        hs = slice(h * HD, (h + 1) * HD)
        frames = reach[0, 0, h, 0] > 0
        rows = reach[0, 0, h, 1] > 0
        zero, neg = jnp.float32(0), jnp.float32(NEG)
        fe_b = jnp.where(frames, zero, neg)
        fo_b = jnp.where(frames & fo_ok, zero, neg)
        p_b = jnp.where(rows, zero, neg)
        o_b = jnp.where(rows & o_ok, zero, neg)
        ok = jnp.where(a_of == 1, fe_b, jnp.where(a_of == 2, fo_b, zero))
        ok = jnp.minimum(ok, jnp.where(b_of == 1, p_b, jnp.where(b_of == 2, o_b, zero)))
        for m, (a, b) in enumerate(TILE_GROUPS):
            qr, kr = slice(a * 16, (b + 1) * 16), slice(m * TILE, (m + 1) * TILE)
            sc[qr, kr] = dot_nt(qs[qr, hs], ks[kr, hs])
            dp[qr, kr] = dot_nt(os_[qr, hs], vs[kr, hs])
        for g in range(GROUPS):
            qr = slice(g * 16, (g + 1) * 16)
            kr = slice(GROUP_TILES[g][0] * TILE, (GROUP_TILES[g][-1] + 1) * TILE)
            bias = jnp.where(jnp.abs(key_group[:, kr] - g) <= 1, ok[:, kr], NEG)
            s = sc[qr, kr] * (scale * LOG2E) + bias
            e = jnp.exp2(s - jnp.max(s, axis=1, keepdims=True))
            p = e * (1.0 / jnp.sum(e, axis=1, keepdims=True))
            d = dp[qr, kr]
            delta = jnp.sum(p * d, axis=1, keepdims=True)
            pb[qr, kr] = p.astype(jnp.bfloat16)
            ds[qr, kr] = (p * ((d - delta) * scale)).astype(jnp.bfloat16)
        aacc[...] = jnp.zeros_like(aacc)
        qacc[...] = jnp.zeros_like(qacc)
        for m, (a, b) in enumerate(TILE_GROUPS):
            qr, kr = slice(a * 16, (b + 1) * 16), slice(m * TILE, (m + 1) * TILE)
            pt, dt = pb[qr, kr], ds[qr, kr]
            gv[kr, hs] = dot_tn(pt, os_[qr, hs])
            gk[kr, hs] = dot_tn(dt, qs[qr, hs])
            aacc[qr] += dot_nn(pt, vs[kr, hs])
            qacc[qr] += dot_nn(dt, ks[kr, hs])
        att[:, hs] = by_row(aacc[...])
        gq[:, hs] = by_row(qacc[...])
    outs = [(gown, 0), (ge, 0), (go, 0), (gfe, 0), (ge, 2), (geo, 0), (gfo, 0), (ge, 4), (gfo_, 0)]
    for slot, (ref, at) in enumerate(outs):
        for j in range(BLOCKS):
            for r in range(2):
                row = j * SPAN + (slot * 2 + r) * 16
                dst = slice(r * W + 16 * j, r * W + 16 * j + 16)
                ref[at, dst] = gk[row : row + 16].astype(ref.dtype)
                ref[at + 1, dst] = gv[row : row + 16].astype(ref.dtype)


def attention(reach, q, o, x, xe, xf, xo, xeo, xfo, xp):
    nframe, nheight = lax.axis_size("frame"), lax.axis_size("height")
    vmem = pl.BlockSpec(memory_space=pltpu.VMEM)
    bf = lambda *shape: jax.ShapeDtypeStruct(shape, jnp.bfloat16)
    fl = lambda *shape: jax.ShapeDtypeStruct(shape, jnp.float32)
    pair = (2, TOK, CHANS)
    return pl.pallas_call(
        functools.partial(attn_kernel, nframe, nheight),
        out_shape=(
            bf(TOK, CHANS), bf(TOK, CHANS), bf(6, TOK, CHANS), bf(*pair), bf(*pair),
            fl(*pair), fl(*pair), fl(*pair), fl(*pair),
        ),
        in_specs=[pl.BlockSpec(memory_space=pltpu.SMEM)] + [vmem] * 9,
        out_specs=(vmem,) * 9,
        scratch_shapes=[
            pltpu.VMEM((TOK, CHANS), jnp.bfloat16),
            pltpu.VMEM((TOK, CHANS), jnp.bfloat16),
            pltpu.VMEM((PADDED, CHANS), jnp.bfloat16),
            pltpu.VMEM((PADDED, CHANS), jnp.bfloat16),
            pltpu.VMEM((TOK, PADDED), jnp.float32),
            pltpu.VMEM((TOK, PADDED), jnp.float32),
            pltpu.VMEM((TOK, PADDED), jnp.bfloat16),
            pltpu.VMEM((TOK, PADDED), jnp.bfloat16),
            pltpu.VMEM((PADDED, CHANS), jnp.float32),
            pltpu.VMEM((PADDED, CHANS), jnp.float32),
            pltpu.VMEM((TOK, HD), jnp.float32),
            pltpu.VMEM((TOK, HD), jnp.float32),
        ],
        compiler_params=pltpu.CompilerParams(vmem_limit_bytes=48 * 1024 * 1024),
        cost_estimate=pl.CostEstimate(
            flops=10 * 160 * 640 * 256, bytes_accessed=4 * 1024 * 1024, transcendentals=160 * 1440
        ),
        name="attention",
    )(reach, q, o, x, xe, xf, xo, xeo, xfo, xp)


def swaps():
    nf, nh = lax.axis_size("frame"), lax.axis_size("height")
    even = lambda i: i ^ 1
    odd = lambda i: ((i + 1) ^ 1) - 1
    along_f = lambda to: [
        (f * nh + h, to(f) * nh + h) for f in range(nf) for h in range(nh) if 0 <= to(f) < nf
    ]
    along_h = lambda to: [
        (f * nh + h, f * nh + to(h)) for f in range(nf) for h in range(nh) if 0 <= to(h) < nh
    ]
    return along_f(even), along_f(odd), along_h(even), along_h(odd)


def local(queries, keys, values, d_out, reach):
    fe, fo, he, ho = swaps()
    swap = lambda array, pairs: lax.ppermute(array, BOTH, pairs)
    shape = queries.shape
    q, o = queries.reshape(TOK, CHANS), d_out.reshape(TOK, CHANS)
    x = jnp.stack([keys.reshape(TOK, CHANS), values.reshape(TOK, CHANS)])
    xo = swap(x, ho)
    xf = swap(x, fo)
    xe = swap(x, fe)
    xfo = swap(xo, fo)
    xeo = swap(xo, fe)
    xp = swap(jnp.concatenate([x, xe, xf]), he)
    att, gq, ge, geo, gfo_, go, gfe, gfo, gown = attention(
        reach, q, o, x, xe, xf, xo, xeo, xfo, xp
    )
    f32, bf16 = jnp.float32, jnp.bfloat16
    rp = swap(ge, he).astype(f32)
    rfo = swap(gfo_, fo).astype(f32)
    reo = swap(geo, fe).astype(f32)
    rf = swap((gfo + rp[4:6]).astype(bf16), fo).astype(f32)
    re = swap((gfe + rp[2:4]).astype(bf16), fe).astype(f32)
    ro = swap((go + rfo + reo).astype(bf16), ho).astype(f32)
    total = (gown + rp[0:2] + rf + re + ro).astype(bf16)
    return (
        att.reshape(shape), gq.reshape(shape), total[0].reshape(shape), total[1].reshape(shape)
    )


def solution(mesh):
    spec = P("frame", "height", None, None)
    return jax.shard_map(
        local, mesh=mesh, in_specs=(spec,) * 5, out_specs=(spec,) * 4, check_vma=False
    )
```

```python
import functools

import jax
import jax.numpy as jnp
from jax import lax
from jax.experimental import pallas as pl
from jax.experimental.pallas import tpu as pltpu
from jax.sharding import PartitionSpec as P

W = 80
WT = 8
GROUPS = W // WT
TOK = 160
HEADS = 2
HD = 128
CHANS = HEADS * HD
BLOCKS = W // 16
TILE = 256
SLOTS = 8
BLOCK = 2 * SLOTS * 16
NEG = -1e30
LOG2E = 1.4426950408889634
SCALE = HD ** (-0.5)
BOTH = ("frame", "height")
F32, BF16 = jnp.float32, jnp.bfloat16


def near(j):
    second = slice(max(2 * j - 1, 0) * 16, (2 * j + 1) * 16)
    first = slice((2 * j + 1) * 16, min(2 * j + 3, GROUPS) * 16)
    return second, first


def dot_nt(a, b):
    return lax.dot_general(a, b, (((1,), (1,)), ((), ())), preferred_element_type=jnp.float32)


def dot_nn(a, b):
    return lax.dot_general(a, b, (((1,), (0,)), ((), ())), preferred_element_type=jnp.float32)


def dot_tn(a, b):
    return lax.dot_general(a, b, (((0,), (0,)), ((), ())), preferred_element_type=jnp.float32)


def by_group(ref):
    wide = ref[...].astype(jnp.float32)
    parts = []
    for g in range(GROUPS):
        for r in range(2):
            parts.append(wide[r * W + g * WT : r * W + (g + 1) * WT])
    return jnp.concatenate(parts, axis=0).astype(jnp.bfloat16)


def by_row(wide):
    parts = []
    for r in range(2):
        for g in range(GROUPS):
            parts.append(wide[g * 16 + r * WT : g * 16 + (r + 1) * WT])
    return jnp.concatenate(parts, axis=0).astype(jnp.bfloat16)


def prepare_kernel(nframe, nheight, reach, q, o, qs, os_, bias):
    qs[...] = by_group(q)
    os_[...] = by_group(o)
    frame, height = lax.axis_index("frame"), lax.axis_index("height")
    fo_ok = (frame > 0) & (frame < nframe - 1)
    o_ok = (height > 0) & (height < nheight - 1)
    slot = lax.broadcasted_iota(jnp.int32, (8, BLOCK), 1) // 32
    at_p = (slot == 1) | (slot == 4) | (slot == 7)
    at_o = (slot == 2) | (slot == 5)
    at_fe = (slot >= 3) & (slot <= 5)
    at_fo = slot >= 6
    corner_row = lax.broadcasted_iota(jnp.int32, (8, BLOCK), 0) == 1
    zero, neg = jnp.float32(0), jnp.float32(NEG)
    for h in range(HEADS):
        frames = reach[0, 0, h, 0] > 0
        rows = reach[0, 0, h, 1] > 0
        fe_b = jnp.where(frames, zero, neg)
        fo_b = jnp.where(frames & fo_ok, zero, neg)
        p_b = jnp.where(rows, zero, neg)
        o_b = jnp.where(rows & o_ok, zero, neg)
        ok = jnp.where(at_fe, fe_b, jnp.where(at_fo, fo_b, zero))
        ok = jnp.minimum(ok, jnp.where(at_p, p_b, jnp.where(at_o, o_b, zero)))
        bias[h] = jnp.where(corner_row, jnp.minimum(fo_b, o_b), ok)


def softmax_kernel(
    qs, os_, bias, x, xf, xe, xo, xfo, xeo, xp,
    gfo_, pm, gm, pc, gc, ks, vs, kc, vc,
    sm, dm, sc, dc,
):
    height = lax.axis_index("height")
    xp = xp.at[1 - lax.rem(height, 2)]
    slots = [(x, 0), (xp, 0), (xo, 0), (xe, 0), (xp, 4), (xeo, 0), (xf, 0), (xp, 2)]
    for j in range(BLOCKS):
        for r in range(2):
            src = slice(r * W + 16 * j, r * W + 16 * j + 16)
            for slot, (ref, at) in enumerate(slots):
                row = j * BLOCK + (slot * 2 + r) * 16
                ks[row : row + 16] = ref[at, src]
                vs[row : row + 16] = ref[at + 1, src]
            row = j * 32 + r * 16
            kc[row : row + 16] = xfo[0, src]
            vc[row : row + 16] = xfo[1, src]
    kc[TOK:] = jnp.zeros((TILE - TOK, CHANS), BF16)
    vc[TOK:] = jnp.zeros((TILE - TOK, CHANS), BF16)

    lane = lax.broadcasted_iota(jnp.int32, (1, BLOCK), 1)
    half = (lane % 16) // WT
    corner_group = jnp.where(lane < TOK, (lane // 32) * 2 + half, 1000)

    for h in range(HEADS):
        hs = slice(h * HD, (h + 1) * HD)
        for j in range(BLOCKS):
            kr = slice(j * BLOCK, (j + 1) * BLOCK)
            second, first = near(j)
            both = slice(second.start, first.stop)
            cut = second.stop - second.start
            for left, right, out in ((qs, ks, sm), (os_, vs, dm)):
                t = dot_nt(left[both, hs], right[kr, hs])
                out[second, BLOCK:] = t[:cut]
                out[first, :BLOCK] = t[cut:]
        sc[...] = dot_nt(qs[:, hs], kc[:, hs])
        dc[...] = dot_nt(os_[:, hs], vc[:, hs])
        ok, corner_ok = bias[h, 0:1], bias[h, 1:2]
        only_last = jnp.where(half == 1, ok, NEG)
        only_first = jnp.where(half == 0, ok, NEG)
        for g in range(GROUPS):
            qr = slice(g * 16, (g + 1) * 16)
            halves = [(slice(0, BLOCK), only_last if g % 2 == 0 else ok)] if g > 0 else []
            if g < GROUPS - 1:
                halves.append((slice(BLOCK, 2 * BLOCK), ok if g % 2 == 0 else only_first))
            corner = jnp.where(jnp.abs(corner_group - g) <= 1, corner_ok, NEG)
            s = [sm[qr, kr] * (SCALE * LOG2E) + add for kr, add in halves]
            s.append(sc[qr] * (SCALE * LOG2E) + corner)
            d = [dm[qr, kr] for kr, _ in halves] + [dc[qr]]
            top = functools.reduce(jnp.maximum, s)
            top = jnp.max(top, axis=1, keepdims=True)
            e = [jnp.exp2(v - top) for v in s]
            inv = 1.0 / jnp.sum(sum(e[1:], e[0]), axis=1, keepdims=True)
            p = [v * inv for v in e]
            pd = [a * b for a, b in zip(p, d)]
            delta = jnp.sum(sum(pd[1:], pd[0]), axis=1, keepdims=True)
            g_s = [((a * (b - delta)) * SCALE).astype(BF16) for a, b in zip(p, d)]
            for (kr, _), a, b in zip(halves, p, g_s):
                pm[h, qr, kr] = a.astype(BF16)
                gm[h, qr, kr] = b
            pc[h, qr] = p[-1].astype(BF16)
            gc[h, qr] = g_s[-1]
        for at, left, right in ((0, gc, qs), (1, pc, os_)):
            t = dot_tn(left[h], right[:, hs]).astype(BF16)
            for j in range(BLOCKS):
                for r in range(2):
                    dst = slice(r * W + 16 * j, r * W + 16 * j + 16)
                    row = j * 32 + r * 16
                    gfo_[at, dst, hs] = t[row : row + 16]


def key_kernel(qs, os_, pm, gm, ge, geo, go, gfe, gfo, gown):
    outs = [(gown, 0), (ge, 0), (go, 0), (gfe, 0), (ge, 2), (geo, 0), (gfo, 0), (ge, 4)]
    for h in range(HEADS):
        hs = slice(h * HD, (h + 1) * HD)
        for j in range(BLOCKS):
            second, first = near(j)
            both = slice(second.start, first.stop)
            for add, left, right in ((0, gm, qs), (1, pm, os_)):
                t = jnp.concatenate([left[h, second, BLOCK:], left[h, first, :BLOCK]], axis=0)
                t = dot_tn(t, right[both, hs])
                for slot, (ref, at) in enumerate(outs):
                    for r in range(2):
                        dst = slice(r * W + 16 * j, r * W + 16 * j + 16)
                        row = (slot * 2 + r) * 16
                        ref[at + add, dst, hs] = t[row : row + 16].astype(ref.dtype)


def query_kernel(ks, vs, kc, vc, pm, gm, pc, gc, att, gq):
    for h in range(HEADS):
        hs = slice(h * HD, (h + 1) * HD)
        for main, corner, right, right_c, out in ((pm, pc, vs, vc, att), (gm, gc, ks, kc, gq)):
            parts = [dot_nn(main[h, :16, BLOCK:], right[:BLOCK, hs])]
            for j in range(1, BLOCKS):
                qr = slice((2 * j - 1) * 16, (2 * j + 1) * 16)
                parts.append(dot_nn(main[h, qr], right[(j - 1) * BLOCK : (j + 1) * BLOCK, hs]))
            parts.append(dot_nn(main[h, TOK - 16 :, :BLOCK], right[(BLOCKS - 1) * BLOCK :, hs]))
            t = jnp.concatenate(parts, axis=0) + dot_nn(corner[h], right_c[:, hs])
            out[:, hs] = by_row(t)


def call(body, name, flops, ins, outs, scratch=(), smem=0):
    vmem = pl.BlockSpec(memory_space=pltpu.VMEM)
    return pl.pallas_call(
        body,
        out_shape=tuple(jax.ShapeDtypeStruct(shape, kind) for shape, kind in outs),
        in_specs=[pl.BlockSpec(memory_space=pltpu.SMEM)] * smem + [vmem] * (len(ins) - smem),
        out_specs=(vmem,) * len(outs),
        scratch_shapes=[pltpu.VMEM(shape, kind) for shape, kind in scratch],
        compiler_params=pltpu.CompilerParams(vmem_limit_bytes=32 * 1024 * 1024),
        cost_estimate=pl.CostEstimate(flops=flops, bytes_accessed=2 * 1024 * 1024, transcendentals=0),
        name=name,
    )(*ins)


def swaps():
    nf, nh = lax.axis_size("frame"), lax.axis_size("height")
    even = lambda i: i ^ 1
    odd = lambda i: ((i + 1) ^ 1) - 1
    along_f = lambda to: [
        (f * nh + h, to(f) * nh + h) for f in range(nf) for h in range(nh) if 0 <= to(f) < nf
    ]
    along_h = lambda to: [
        (f * nh + h, f * nh + to(h)) for f in range(nf) for h in range(nh) if 0 <= to(h) < nh
    ]
    return along_f(even), along_f(odd), along_h(even), along_h(odd)


def local(queries, keys, values, d_out, reach):
    fe, fo, he, ho = swaps()
    swap = lambda array, pairs: lax.ppermute(array, BOTH, pairs)
    chip = [list(pair) for pair in he if pair[0] < pair[1]]
    share = lambda v: lax.all_gather(v, BOTH, axis_index_groups=chip)
    nframe, nheight = lax.axis_size("frame"), lax.axis_size("height")
    shape = queries.shape
    tile, pair = (TOK, CHANS), (2, TOK, CHANS)
    q, o = queries.reshape(tile), d_out.reshape(tile)
    x = jnp.stack([keys.reshape(tile), values.reshape(tile)])
    xf = swap(x, fo)
    xo = swap(x, ho)
    xe = swap(x, fe)
    xfo = swap(xo, fo)
    xeo = swap(xo, fe)
    xp = share(jnp.concatenate([x, xf, xe]))
    keys_all, keys_corner = (BLOCKS * BLOCK, CHANS), (TILE, CHANS)
    main, corner = (HEADS, TOK, 2 * BLOCK), (HEADS, TOK, TILE)
    qs, os_, bias = call(
        functools.partial(prepare_kernel, nframe, nheight), "prepare", 10**8, (reach, q, o),
        [(tile, BF16)] * 2 + [((HEADS, 8, BLOCK), F32)], (), 1,
    )
    gfo_, pm, gm, pc, gc, ks, vs, kc, vc = call(
        softmax_kernel, "softmax", 2 * 10**9, (qs, os_, bias, x, xf, xe, xo, xfo, xeo, xp),
        [(pair, BF16)] + [(main, BF16)] * 2 + [(corner, BF16)] * 2
        + [(keys_all, BF16)] * 2 + [(keys_corner, BF16)] * 2,
        [((TOK, 2 * BLOCK), F32)] * 2 + [((TOK, TILE), F32)] * 2,
    )
    ge, geo, go, gfe, gfo, gown = call(
        key_kernel, "keys", 10**9, (qs, os_, pm, gm),
        [((6, TOK, CHANS), BF16), (pair, BF16)] + [(pair, F32)] * 4,
    )
    att, gq = call(
        query_kernel, "queries", 10**9, (ks, vs, kc, vc, pm, gm, pc, gc), [(tile, BF16)] * 2
    )
    other = 1 - lax.axis_index("height") % 2
    rp = lax.dynamic_index_in_dim(share(ge), other, 0, False).astype(F32)
    rco = swap(gfo_, ho).astype(F32)
    reo = swap(geo, fe).astype(F32)
    to_fo = (gfo + rp[4:6] + rco).astype(BF16)
    to_fo, gfe, go = lax.optimization_barrier((to_fo, gfe, go))
    rf = swap(to_fo, fo).astype(F32)
    re = swap((gfe + rp[2:4]).astype(BF16), fe).astype(F32)
    ro = swap((go + reo).astype(BF16), ho).astype(F32)
    total = (gown + rp[0:2] + ro + re + rf).astype(BF16)
    return (
        att.reshape(shape), gq.reshape(shape), total[0].reshape(shape), total[1].reshape(shape)
    )


def solution(mesh):
    spec = P("frame", "height", None, None)
    return jax.shard_map(
        local, mesh=mesh, in_specs=(spec,) * 5, out_specs=(spec,) * 4, check_vma=False
    )
```

```python
import functools

import jax
import jax.numpy as jnp
from jax import lax
from jax.experimental import pallas as pl
from jax.experimental.pallas import tpu as pltpu
from jax.sharding import PartitionSpec as P

W = 80
WT = 8
GROUPS = W // WT
TOK = 160
HEADS = 2
HD = 128
CHANS = HEADS * HD
BLOCKS = W // 16
TILE = 256
SLOTS = 8
BLOCK = 2 * SLOTS * 16
NEG = -1e30
LOG2E = 1.4426950408889634
SCALE = HD ** (-0.5)
BOTH = ("frame", "height")
F32, BF16 = jnp.float32, jnp.bfloat16


def near(j):
    second = slice(max(2 * j - 1, 0) * 16, (2 * j + 1) * 16)
    first = slice((2 * j + 1) * 16, min(2 * j + 3, GROUPS) * 16)
    return second, first


def dot_nt(a, b):
    return lax.dot_general(a, b, (((1,), (1,)), ((), ())), preferred_element_type=jnp.float32)


def dot_nn(a, b):
    return lax.dot_general(a, b, (((1,), (0,)), ((), ())), preferred_element_type=jnp.float32)


def dot_tn(a, b):
    return lax.dot_general(a, b, (((0,), (0,)), ((), ())), preferred_element_type=jnp.float32)


def by_group(ref):
    wide = ref[...].astype(jnp.float32)
    parts = []
    for g in range(GROUPS):
        for r in range(2):
            parts.append(wide[r * W + g * WT : r * W + (g + 1) * WT])
    return jnp.concatenate(parts, axis=0).astype(jnp.bfloat16)


def by_row(wide):
    parts = []
    for r in range(2):
        for g in range(GROUPS):
            parts.append(wide[g * 16 + r * WT : g * 16 + (r + 1) * WT])
    return jnp.concatenate(parts, axis=0).astype(jnp.bfloat16)


def prepare_kernel(nframe, nheight, reach, q, o, qs, os_, bias):
    qs[...] = by_group(q)
    os_[...] = by_group(o)
    frame, height = lax.axis_index("frame"), lax.axis_index("height")
    fo_ok = (frame > 0) & (frame < nframe - 1)
    o_ok = (height > 0) & (height < nheight - 1)
    slot = lax.broadcasted_iota(jnp.int32, (8, BLOCK), 1) // 32
    at_p = (slot == 1) | (slot == 4) | (slot == 7)
    at_o = (slot == 2) | (slot == 5)
    at_fe = (slot >= 3) & (slot <= 5)
    at_fo = slot >= 6
    corner_row = lax.broadcasted_iota(jnp.int32, (8, BLOCK), 0) == 1
    zero, neg = jnp.float32(0), jnp.float32(NEG)
    for h in range(HEADS):
        frames = reach[0, 0, h, 0] > 0
        rows = reach[0, 0, h, 1] > 0
        fe_b = jnp.where(frames, zero, neg)
        fo_b = jnp.where(frames & fo_ok, zero, neg)
        p_b = jnp.where(rows, zero, neg)
        o_b = jnp.where(rows & o_ok, zero, neg)
        ok = jnp.where(at_fe, fe_b, jnp.where(at_fo, fo_b, zero))
        ok = jnp.minimum(ok, jnp.where(at_p, p_b, jnp.where(at_o, o_b, zero)))
        bias[h] = jnp.where(corner_row, jnp.minimum(fo_b, o_b), ok)


def softmax_kernel(
    qs, os_, bias, x, xf, xe, xo, xeo, xfo, xp,
    gfo_, pm, gm, pc, gc, ks, vs, kc, vc,
    sm, dm, sc, dc,
):
    height = lax.axis_index("height")
    xp = xp.at[1 - lax.rem(height, 2)]
    slots = [(x, 0), (xp, 0), (xo, 0), (xe, 0), (xp, 4), (xeo, 0), (xf, 0), (xp, 2)]
    for j in range(BLOCKS):
        for r in range(2):
            src = slice(r * W + 16 * j, r * W + 16 * j + 16)
            for slot, (ref, at) in enumerate(slots):
                row = j * BLOCK + (slot * 2 + r) * 16
                ks[row : row + 16] = ref[at, src]
                vs[row : row + 16] = ref[at + 1, src]
            row = j * 32 + r * 16
            kc[row : row + 16] = xfo[0, src]
            vc[row : row + 16] = xfo[1, src]
    kc[TOK:] = jnp.zeros((TILE - TOK, CHANS), BF16)
    vc[TOK:] = jnp.zeros((TILE - TOK, CHANS), BF16)

    lane = lax.broadcasted_iota(jnp.int32, (1, BLOCK), 1)
    half = (lane % 16) // WT
    corner_group = jnp.where(lane < TOK, (lane // 32) * 2 + half, 1000)

    for h in range(HEADS):
        hs = slice(h * HD, (h + 1) * HD)
        for j in range(BLOCKS):
            kr = slice(j * BLOCK, (j + 1) * BLOCK)
            second, first = near(j)
            both = slice(second.start, first.stop)
            cut = second.stop - second.start
            for left, right, out in ((qs, ks, sm), (os_, vs, dm)):
                t = dot_nt(left[both, hs], right[kr, hs])
                out[second, BLOCK:] = t[:cut]
                out[first, :BLOCK] = t[cut:]
        sc[...] = dot_nt(qs[:, hs], kc[:, hs])
        dc[...] = dot_nt(os_[:, hs], vc[:, hs])
        ok, corner_ok = bias[h, 0:1], bias[h, 1:2]
        only_last = jnp.where(half == 1, ok, NEG)
        only_first = jnp.where(half == 0, ok, NEG)
        for g in range(GROUPS):
            qr = slice(g * 16, (g + 1) * 16)
            halves = [(slice(0, BLOCK), only_last if g % 2 == 0 else ok)] if g > 0 else []
            if g < GROUPS - 1:
                halves.append((slice(BLOCK, 2 * BLOCK), ok if g % 2 == 0 else only_first))
            corner = jnp.where(jnp.abs(corner_group - g) <= 1, corner_ok, NEG)
            s = [sm[qr, kr] * (SCALE * LOG2E) + add for kr, add in halves]
            s.append(sc[qr] * (SCALE * LOG2E) + corner)
            d = [dm[qr, kr] for kr, _ in halves] + [dc[qr]]
            top = functools.reduce(jnp.maximum, s)
            top = jnp.max(top, axis=1, keepdims=True)
            e = [jnp.exp2(v - top) for v in s]
            inv = 1.0 / jnp.sum(sum(e[1:], e[0]), axis=1, keepdims=True)
            p = [v * inv for v in e]
            pd = [a * b for a, b in zip(p, d)]
            delta = jnp.sum(sum(pd[1:], pd[0]), axis=1, keepdims=True)
            g_s = [((a * (b - delta)) * SCALE).astype(BF16) for a, b in zip(p, d)]
            for (kr, _), a, b in zip(halves, p, g_s):
                pm[h, qr, kr] = a.astype(BF16)
                gm[h, qr, kr] = b
            pc[h, qr] = p[-1].astype(BF16)
            gc[h, qr] = g_s[-1]
        for at, left, right in ((0, gc, qs), (1, pc, os_)):
            t = dot_tn(left[h], right[:, hs]).astype(BF16)
            for j in range(BLOCKS):
                for r in range(2):
                    dst = slice(r * W + 16 * j, r * W + 16 * j + 16)
                    row = j * 32 + r * 16
                    gfo_[at, dst, hs] = t[row : row + 16]


def key_kernel(qs, os_, pm, gm, ge, geo, go, gfe, gfo, gown):
    outs = [(gown, 0), (ge, 0), (go, 0), (gfe, 0), (ge, 2), (geo, 0), (gfo, 0), (ge, 4)]
    for h in range(HEADS):
        hs = slice(h * HD, (h + 1) * HD)
        for j in range(BLOCKS):
            second, first = near(j)
            both = slice(second.start, first.stop)
            for add, left, right in ((0, gm, qs), (1, pm, os_)):
                t = jnp.concatenate([left[h, second, BLOCK:], left[h, first, :BLOCK]], axis=0)
                t = dot_tn(t, right[both, hs])
                for slot, (ref, at) in enumerate(outs):
                    for r in range(2):
                        dst = slice(r * W + 16 * j, r * W + 16 * j + 16)
                        row = (slot * 2 + r) * 16
                        ref[at + add, dst, hs] = t[row : row + 16].astype(ref.dtype)


def query_kernel(ks, vs, kc, vc, pm, gm, pc, gc, att, gq):
    for h in range(HEADS):
        hs = slice(h * HD, (h + 1) * HD)
        for main, corner, right, right_c, out in ((pm, pc, vs, vc, att), (gm, gc, ks, kc, gq)):
            parts = [dot_nn(main[h, :16, BLOCK:], right[:BLOCK, hs])]
            for j in range(1, BLOCKS):
                qr = slice((2 * j - 1) * 16, (2 * j + 1) * 16)
                parts.append(dot_nn(main[h, qr], right[(j - 1) * BLOCK : (j + 1) * BLOCK, hs]))
            parts.append(dot_nn(main[h, TOK - 16 :, :BLOCK], right[(BLOCKS - 1) * BLOCK :, hs]))
            t = jnp.concatenate(parts, axis=0) + dot_nn(corner[h], right_c[:, hs])
            out[:, hs] = by_row(t)


def call(body, name, flops, ins, outs, scratch=(), smem=0):
    vmem = pl.BlockSpec(memory_space=pltpu.VMEM)
    return pl.pallas_call(
        body,
        out_shape=tuple(jax.ShapeDtypeStruct(shape, kind) for shape, kind in outs),
        in_specs=[pl.BlockSpec(memory_space=pltpu.SMEM)] * smem + [vmem] * (len(ins) - smem),
        out_specs=(vmem,) * len(outs),
        scratch_shapes=[pltpu.VMEM(shape, kind) for shape, kind in scratch],
        compiler_params=pltpu.CompilerParams(vmem_limit_bytes=32 * 1024 * 1024),
        cost_estimate=pl.CostEstimate(flops=flops, bytes_accessed=2 * 1024 * 1024, transcendentals=0),
        name=name,
    )(*ins)


def swaps():
    nf, nh = lax.axis_size("frame"), lax.axis_size("height")
    even = lambda i: i ^ 1
    odd = lambda i: ((i + 1) ^ 1) - 1
    along_f = lambda to: [
        (f * nh + h, to(f) * nh + h) for f in range(nf) for h in range(nh) if 0 <= to(f) < nf
    ]
    along_h = lambda to: [
        (f * nh + h, f * nh + to(h)) for f in range(nf) for h in range(nh) if 0 <= to(h) < nh
    ]
    return along_f(even), along_f(odd), along_h(even), along_h(odd)


def local(queries, keys, values, d_out, reach):
    fe, fo, he, ho = swaps()
    swap = lambda array, pairs: lax.ppermute(array, BOTH, pairs)
    chip = [list(pair) for pair in he if pair[0] < pair[1]]
    share = lambda v: lax.all_gather(v, BOTH, axis_index_groups=chip)
    nframe, nheight = lax.axis_size("frame"), lax.axis_size("height")
    shape = queries.shape
    tile, pair = (TOK, CHANS), (2, TOK, CHANS)
    q, o = queries.reshape(tile), d_out.reshape(tile)
    x = jnp.stack([keys.reshape(tile), values.reshape(tile)])
    xf = swap(x, fo)
    xo = swap(x, ho)
    xe = swap(x, fe)
    xeo = swap(xo, fe)
    xfo = swap(xf, ho)
    xp = share(jnp.concatenate([x, xf, xe]))
    keys_all, keys_corner = (BLOCKS * BLOCK, CHANS), (TILE, CHANS)
    main, corner = (HEADS, TOK, 2 * BLOCK), (HEADS, TOK, TILE)
    qs, os_, bias = call(
        functools.partial(prepare_kernel, nframe, nheight), "prepare", 10**8, (reach, q, o),
        [(tile, BF16)] * 2 + [((HEADS, 8, BLOCK), F32)], (), 1,
    )
    gfo_, pm, gm, pc, gc, ks, vs, kc, vc = call(
        softmax_kernel, "softmax", 2 * 10**9, (qs, os_, bias, x, xf, xe, xo, xeo, xfo, xp),
        [(pair, BF16)] + [(main, BF16)] * 2 + [(corner, BF16)] * 2
        + [(keys_all, BF16)] * 2 + [(keys_corner, BF16)] * 2,
        [((TOK, 2 * BLOCK), F32)] * 2 + [((TOK, TILE), F32)] * 2,
    )
    ge, geo, go, gfe, gfo, gown = call(
        key_kernel, "keys", 10**9, (qs, os_, pm, gm),
        [((6, TOK, CHANS), BF16), (pair, BF16)] + [(pair, F32)] * 4,
    )
    att, gq = call(
        query_kernel, "queries", 10**9, (ks, vs, kc, vc, pm, gm, pc, gc), [(tile, BF16)] * 2
    )
    other = 1 - lax.axis_index("height") % 2
    rp = lax.dynamic_index_in_dim(share(ge), other, 0, False).astype(F32)
    rco = swap(gfo_, ho).astype(F32)
    reo = swap(geo, fe).astype(F32)
    to_fo = (gfo + rp[4:6] + rco).astype(BF16)
    to_fo, gfe, go = lax.optimization_barrier((to_fo, gfe, go))
    rf = swap(to_fo, fo).astype(F32)
    re = swap((gfe + rp[2:4]).astype(BF16), fe).astype(F32)
    ro = swap((go + reo).astype(BF16), ho).astype(F32)
    total = (gown + rp[0:2] + ro + re + rf).astype(BF16)
    return (
        att.reshape(shape), gq.reshape(shape), total[0].reshape(shape), total[1].reshape(shape)
    )


def solution(mesh):
    spec = P("frame", "height", None, None)
    return jax.shard_map(
        local, mesh=mesh, in_specs=(spec,) * 5, out_specs=(spec,) * 4, check_vma=False
    )
```

```python
import functools

import jax
import jax.numpy as jnp
from jax import lax
from jax.experimental import pallas as pl
from jax.experimental.pallas import tpu as pltpu
from jax.sharding import PartitionSpec as P

W = 80
WT = 8
GROUPS = W // WT
TOK = 160
HEADS = 2
HD = 128
CHANS = HEADS * HD
BLOCKS = W // 16
TILE = 256
SLOTS = 8
BLOCK = 2 * SLOTS * 16
NEG = -1e30
LOG2E = 1.4426950408889634
SCALE = HD ** (-0.5)
BOTH = ("frame", "height")
F32, BF16 = jnp.float32, jnp.bfloat16


def near(j):
    second = slice(max(2 * j - 1, 0) * 16, (2 * j + 1) * 16)
    first = slice((2 * j + 1) * 16, min(2 * j + 3, GROUPS) * 16)
    return second, first


def dot_nt(a, b):
    return lax.dot_general(a, b, (((1,), (1,)), ((), ())), preferred_element_type=jnp.float32)


def dot_nn(a, b):
    return lax.dot_general(a, b, (((1,), (0,)), ((), ())), preferred_element_type=jnp.float32)


def dot_tn(a, b):
    return lax.dot_general(a, b, (((0,), (0,)), ((), ())), preferred_element_type=jnp.float32)


def by_group(ref):
    wide = ref[...].astype(jnp.float32)
    parts = []
    for g in range(GROUPS):
        for r in range(2):
            parts.append(wide[r * W + g * WT : r * W + (g + 1) * WT])
    return jnp.concatenate(parts, axis=0).astype(jnp.bfloat16)


def by_row(wide):
    parts = []
    for r in range(2):
        for g in range(GROUPS):
            parts.append(wide[g * 16 + r * WT : g * 16 + (r + 1) * WT])
    return jnp.concatenate(parts, axis=0).astype(jnp.bfloat16)


def prepare_kernel(nframe, nheight, reach, q, o, qs, os_, bias):
    qs[...] = by_group(q)
    os_[...] = by_group(o)
    frame, height = lax.axis_index("frame"), lax.axis_index("height")
    fo_ok = (frame > 0) & (frame < nframe - 1)
    o_ok = (height > 0) & (height < nheight - 1)
    slot = lax.broadcasted_iota(jnp.int32, (8, BLOCK), 1) // 32
    at_p = (slot == 1) | (slot == 4) | (slot == 7)
    at_o = (slot == 2) | (slot == 5)
    at_fe = (slot >= 3) & (slot <= 5)
    at_fo = slot >= 6
    corner_row = lax.broadcasted_iota(jnp.int32, (8, BLOCK), 0) == 1
    zero, neg = jnp.float32(0), jnp.float32(NEG)
    for h in range(HEADS):
        frames = reach[0, 0, h, 0] > 0
        rows = reach[0, 0, h, 1] > 0
        fe_b = jnp.where(frames, zero, neg)
        fo_b = jnp.where(frames & fo_ok, zero, neg)
        p_b = jnp.where(rows, zero, neg)
        o_b = jnp.where(rows & o_ok, zero, neg)
        ok = jnp.where(at_fe, fe_b, jnp.where(at_fo, fo_b, zero))
        ok = jnp.minimum(ok, jnp.where(at_p, p_b, jnp.where(at_o, o_b, zero)))
        bias[h] = jnp.where(corner_row, jnp.minimum(fo_b, o_b), ok)


def softmax_kernel(
    qs, os_, bias, x, xf, xe, xo, xeo, xfo, xp,
    gfo_, pm, gm, pc, gc, ks, vs, kc, vc,
    sm, dm, sc, dc,
):
    height = lax.axis_index("height")
    xp = xp.at[1 - lax.rem(height, 2)]
    slots = [(x, 0), (xp, 0), (xo, 0), (xe, 0), (xp, 4), (xeo, 0), (xf, 0), (xp, 2)]
    for j in range(BLOCKS):
        for r in range(2):
            src = slice(r * W + 16 * j, r * W + 16 * j + 16)
            for slot, (ref, at) in enumerate(slots):
                row = j * BLOCK + (slot * 2 + r) * 16
                ks[row : row + 16] = ref[at, src]
                vs[row : row + 16] = ref[at + 1, src]
            row = j * 32 + r * 16
            kc[row : row + 16] = xfo[0, src]
            vc[row : row + 16] = xfo[1, src]
    kc[TOK:] = jnp.zeros((TILE - TOK, CHANS), BF16)
    vc[TOK:] = jnp.zeros((TILE - TOK, CHANS), BF16)

    lane = lax.broadcasted_iota(jnp.int32, (1, BLOCK), 1)
    half = (lane % 16) // WT
    corner_group = jnp.where(lane < TOK, (lane // 32) * 2 + half, 1000)

    for h in range(HEADS):
        hs = slice(h * HD, (h + 1) * HD)
        for j in range(BLOCKS):
            kr = slice(j * BLOCK, (j + 1) * BLOCK)
            second, first = near(j)
            both = slice(second.start, first.stop)
            cut = second.stop - second.start
            for left, right, out in ((qs, ks, sm), (os_, vs, dm)):
                t = dot_nt(left[both, hs], right[kr, hs])
                out[second, BLOCK:] = t[:cut]
                out[first, :BLOCK] = t[cut:]
        sc[...] = dot_nt(qs[:, hs], kc[:, hs])
        dc[...] = dot_nt(os_[:, hs], vc[:, hs])
        ok, corner_ok = bias[h, 0:1], bias[h, 1:2]
        only_last = jnp.where(half == 1, ok, NEG)
        only_first = jnp.where(half == 0, ok, NEG)
        for g in range(GROUPS):
            qr = slice(g * 16, (g + 1) * 16)
            halves = [(slice(0, BLOCK), only_last if g % 2 == 0 else ok)] if g > 0 else []
            if g < GROUPS - 1:
                halves.append((slice(BLOCK, 2 * BLOCK), ok if g % 2 == 0 else only_first))
            corner = jnp.where(jnp.abs(corner_group - g) <= 1, corner_ok, NEG)
            s = [sm[qr, kr] * (SCALE * LOG2E) + add for kr, add in halves]
            s.append(sc[qr] * (SCALE * LOG2E) + corner)
            d = [dm[qr, kr] for kr, _ in halves] + [dc[qr]]
            top = functools.reduce(jnp.maximum, s)
            top = jnp.max(top, axis=1, keepdims=True)
            e = [jnp.exp2(v - top) for v in s]
            inv = 1.0 / jnp.sum(sum(e[1:], e[0]), axis=1, keepdims=True)
            p = [v * inv for v in e]
            pd = [a * b for a, b in zip(p, d)]
            delta = jnp.sum(sum(pd[1:], pd[0]), axis=1, keepdims=True)
            g_s = [((a * (b - delta)) * SCALE).astype(BF16) for a, b in zip(p, d)]
            for (kr, _), a, b in zip(halves, p, g_s):
                pm[h, qr, kr] = a.astype(BF16)
                gm[h, qr, kr] = b
            pc[h, qr] = p[-1].astype(BF16)
            gc[h, qr] = g_s[-1]
        for at, left, right in ((0, gc, qs), (1, pc, os_)):
            t = dot_tn(left[h], right[:, hs]).astype(BF16)
            for j in range(BLOCKS):
                for r in range(2):
                    dst = slice(r * W + 16 * j, r * W + 16 * j + 16)
                    row = j * 32 + r * 16
                    gfo_[at, dst, hs] = t[row : row + 16]


def key_kernel(qs, os_, pm, gm, ge, geo, go, gfe, gfo, gown):
    outs = [(gown, 0), (ge, 0), (go, 0), (gfe, 0), (ge, 2), (geo, 0), (gfo, 0), (ge, 4)]
    for h in range(HEADS):
        hs = slice(h * HD, (h + 1) * HD)
        for j in range(BLOCKS):
            second, first = near(j)
            both = slice(second.start, first.stop)
            for add, left, right in ((0, gm, qs), (1, pm, os_)):
                t = jnp.concatenate([left[h, second, BLOCK:], left[h, first, :BLOCK]], axis=0)
                t = dot_tn(t, right[both, hs])
                for slot, (ref, at) in enumerate(outs):
                    for r in range(2):
                        dst = slice(r * W + 16 * j, r * W + 16 * j + 16)
                        row = (slot * 2 + r) * 16
                        ref[at + add, dst, hs] = t[row : row + 16].astype(ref.dtype)


def query_kernel(ks, vs, kc, vc, pm, gm, pc, gc, att, gq):
    for h in range(HEADS):
        hs = slice(h * HD, (h + 1) * HD)
        for main, corner, right, right_c, out in ((pm, pc, vs, vc, att), (gm, gc, ks, kc, gq)):
            parts = [dot_nn(main[h, :16, BLOCK:], right[:BLOCK, hs])]
            for j in range(1, BLOCKS):
                qr = slice((2 * j - 1) * 16, (2 * j + 1) * 16)
                parts.append(dot_nn(main[h, qr], right[(j - 1) * BLOCK : (j + 1) * BLOCK, hs]))
            parts.append(dot_nn(main[h, TOK - 16 :, :BLOCK], right[(BLOCKS - 1) * BLOCK :, hs]))
            t = jnp.concatenate(parts, axis=0) + dot_nn(corner[h], right_c[:, hs])
            out[:, hs] = by_row(t)


def call(body, name, flops, ins, outs, scratch=(), smem=0):
    vmem = pl.BlockSpec(memory_space=pltpu.VMEM)
    return pl.pallas_call(
        body,
        out_shape=tuple(jax.ShapeDtypeStruct(shape, kind) for shape, kind in outs),
        in_specs=[pl.BlockSpec(memory_space=pltpu.SMEM)] * smem + [vmem] * (len(ins) - smem),
        out_specs=(vmem,) * len(outs),
        scratch_shapes=[pltpu.VMEM(shape, kind) for shape, kind in scratch],
        compiler_params=pltpu.CompilerParams(vmem_limit_bytes=32 * 1024 * 1024),
        cost_estimate=pl.CostEstimate(flops=flops, bytes_accessed=2 * 1024 * 1024, transcendentals=0),
        name=name,
    )(*ins)


def swaps():
    nf, nh = lax.axis_size("frame"), lax.axis_size("height")
    even = lambda i: i ^ 1
    odd = lambda i: ((i + 1) ^ 1) - 1
    along_f = lambda to: [
        (f * nh + h, to(f) * nh + h) for f in range(nf) for h in range(nh) if 0 <= to(f) < nf
    ]
    along_h = lambda to: [
        (f * nh + h, f * nh + to(h)) for f in range(nf) for h in range(nh) if 0 <= to(h) < nh
    ]
    return along_f(even), along_f(odd), along_h(even), along_h(odd)


def local(queries, keys, values, d_out, reach):
    fe, fo, he, ho = swaps()
    swap = lambda array, pairs: lax.ppermute(array, BOTH, pairs)
    chip = [list(pair) for pair in he if pair[0] < pair[1]]
    share = lambda v: lax.all_gather(v, BOTH, axis_index_groups=chip)
    nframe, nheight = lax.axis_size("frame"), lax.axis_size("height")
    shape = queries.shape
    tile, pair = (TOK, CHANS), (2, TOK, CHANS)
    q, o = queries.reshape(tile), d_out.reshape(tile)
    x = jnp.stack([keys.reshape(tile), values.reshape(tile)])
    xf = swap(x, fo)
    xo = swap(x, ho)
    xe = swap(x, fe)
    xeo = swap(xo, fe)
    xfo = swap(xf, ho)
    xp = share(jnp.concatenate([x, xf, xe]))
    keys_all, keys_corner = (BLOCKS * BLOCK, CHANS), (TILE, CHANS)
    main, corner = (HEADS, TOK, 2 * BLOCK), (HEADS, TOK, TILE)
    reach, q, o, xeo = lax.optimization_barrier((reach, q, o, xeo))
    qs, os_, bias = call(
        functools.partial(prepare_kernel, nframe, nheight), "prepare", 10**8, (reach, q, o),
        [(tile, BF16)] * 2 + [((HEADS, 8, BLOCK), F32)], (), 1,
    )
    gfo_, pm, gm, pc, gc, ks, vs, kc, vc = call(
        softmax_kernel, "softmax", 2 * 10**9, (qs, os_, bias, x, xf, xe, xo, xeo, xfo, xp),
        [(pair, BF16)] + [(main, BF16)] * 2 + [(corner, BF16)] * 2
        + [(keys_all, BF16)] * 2 + [(keys_corner, BF16)] * 2,
        [((TOK, 2 * BLOCK), F32)] * 2 + [((TOK, TILE), F32)] * 2,
    )
    ge, geo, go, gfe, gfo, gown = call(
        key_kernel, "keys", 10**9, (qs, os_, pm, gm),
        [((6, TOK, CHANS), BF16), (pair, BF16)] + [(pair, F32)] * 4,
    )
    att, gq = call(
        query_kernel, "queries", 10**9, (ks, vs, kc, vc, pm, gm, pc, gc), [(tile, BF16)] * 2
    )
    other = 1 - lax.axis_index("height") % 2
    rp = lax.dynamic_index_in_dim(share(ge), other, 0, False).astype(F32)
    rco = swap(gfo_, ho).astype(F32)
    reo = swap(geo, fe).astype(F32)
    to_fo = (gfo + rp[4:6] + rco).astype(BF16)
    to_fo, gfe, go = lax.optimization_barrier((to_fo, gfe, go))
    rf = swap(to_fo, fo).astype(F32)
    re = swap((gfe + rp[2:4]).astype(BF16), fe).astype(F32)
    ro = swap((go + reo).astype(BF16), ho).astype(F32)
    total = (gown + rp[0:2] + ro + re + rf).astype(BF16)
    return (
        att.reshape(shape), gq.reshape(shape), total[0].reshape(shape), total[1].reshape(shape)
    )


def solution(mesh):
    spec = P("frame", "height", None, None)
    return jax.shard_map(
        local, mesh=mesh, in_specs=(spec,) * 5, out_specs=(spec,) * 4, check_vma=False
    )
```
